512 devices in a mesh: rows: 32 (over x, y, core), cols: 16 (over z).
Axes of the slice: x: 4, y: 4, z: 16, core: 2. Of those that a mesh axis runs over, the one named last changes fastest.
Arguments:
- images: bfloat16 [2, 3, 2048, 8192], P(None, None, 'rows', 'cols'), may hold values from -6 to 6
- enc_weight: bfloat16 [3, 8, 8, 128], replicated, may hold values from -0.4375 to 0.4375
- enc_bias: float32 [128], replicated, may hold values from -3 to 3
- mix_weight: bfloat16 [3, 3, 128, 128], replicated, may hold values from -0.1875 to 0.1875
- mix_bias: float32 [128], replicated, may hold values from -3 to 3
- agg_weight: bfloat16 [3, 3, 256, 128], replicated, may hold values from -0.125 to 0.125
- agg_bias: float32 [128], replicated, may hold values from -3 to 3
Outputs:
- aggregated: bfloat16 [512, 2048, 128], P(('rows', 'cols'))
The draws below stay inside these ranges and needn't reach their ends.
All inputs are finite; a program needn't handle non-finite values.
Results may differ from the reference program's by a relative error of at most 0.0055.
Values may be sent and summed in bfloat16 or wider, within the bound.
A program may use at most 64 MiB of HBM per device.

```python
import math
import jax
import jax.numpy as jnp
from jax import lax

CIN = 3
CH = 128
DISP = 256
AGG = 128
FWIDTH = 2048
FHEIGHT = 512


def block_levels(stream_key, extent, cuts, least, top_value):
    gain, own = 1.0, jax.random.fold_in(stream_key, 6)
    for dim, blocks in cuts:
        heights = jnp.exp(jax.random.uniform(jax.random.fold_in(own, dim), (blocks,), jnp.float32, least / len(cuts), top_value / len(cuts)))
        gain = gain * jnp.repeat(heights, extent[dim] // blocks).reshape([-1 if axis == dim else 1 for axis in range(len(extent))])
    return gain


def gaussian(rng, extent, spread, limit, split=(), held_as=jnp.bfloat16):
    level = block_levels(rng, extent, split, -0.22, 0.18) if split else 1.0
    drawn = jax.random.normal(rng, extent, jnp.float32) * spread * level
    return jnp.minimum(jnp.maximum(drawn, -limit), limit).astype(held_as)


def setup_inputs(seed: int = 0) -> dict:
    splits = jax.random.split(jax.random.key(seed), 8)
    return {
        "images": gaussian(splits[0], (2, CIN, 4 * FHEIGHT, 4 * FWIDTH), 1.0, 6.0, ((2, 32), (3, 16))),
        "enc_weight": gaussian(splits[1], (CIN, 8, 8, CH), (CIN * 64) ** -0.5, 0.4375),
        "enc_bias": gaussian(splits[2], (CH,), 0.5, 3.0, (), jnp.float32),
        "mix_weight": gaussian(splits[3], (3, 3, CH, CH), (9 * CH) ** -0.5, 0.1875),
        "mix_bias": gaussian(splits[4], (CH,), 0.5, 3.0, (), jnp.float32),
        "agg_weight": gaussian(splits[5], (3, 3, DISP, AGG), (9 * DISP) ** -0.5, 0.125),
        "agg_bias": gaussian(splits[6], (AGG,), 0.5, 3.0, (), jnp.float32),
    }


def correlate(left, right_ext):
    rows_n, width, chans = left.shape
    block = DISP // 2
    count = width // block
    left_blocks = left.reshape(rows_n, count, block, chans)
    pieces = [right_ext[:, j * block:j * block + width].reshape(rows_n, count, block, chans) for j in range(DISP // block + 1)]
    window = jnp.concatenate(pieces, axis=2)
    scores = jnp.einsum('rbic,rbjc->rbij', left_blocks.astype(jnp.float32), window.astype(jnp.float32))
    scores = (scores * (1.0 / math.sqrt(chans))).astype(jnp.bfloat16)
    flat = scores.reshape(rows_n, count, block * (block + DISP))
    flat = jnp.pad(flat, ((0, 0), (0, 0), (0, block)))
    skew = flat.reshape(rows_n, count, block, block + DISP + 1)[..., 1:DISP + 1]
    return jnp.flip(skew, axis=-1).reshape(rows_n, width, DISP)

def reference(images, enc_weight, enc_bias, mix_weight, mix_bias, agg_weight, agg_bias):
    first = lax.conv_general_dilated(images.astype(jnp.float32), enc_weight.astype(jnp.float32), (4, 4), ((2, 2), (2, 2)), dimension_numbers=('NCHW', 'IHWO', 'NHWC'), precision=lax.Precision.HIGHEST)
    lower = jnp.maximum(first + enc_bias, 0.0).astype(jnp.bfloat16)
    mixed = lax.conv_general_dilated(lower.astype(jnp.float32), mix_weight.astype(jnp.float32), (1, 1), ((1, 1), (1, 1)), dimension_numbers=('NHWC', 'HWIO', 'NHWC'), precision=lax.Precision.HIGHEST)
    feats = (lower.astype(jnp.float32) + mixed + mix_bias).astype(jnp.bfloat16)
    height = feats.shape[1]
    width = feats.shape[2]
    right_pad = jnp.pad(feats[1], ((0, 0), (DISP, 0), (0, 0)))

    def one_row(index):
        left_row = lax.dynamic_slice_in_dim(feats[0], index, 1, 0)
        right_row = lax.dynamic_slice_in_dim(right_pad, index, 1, 0)
        return correlate(left_row, right_row)[0]
    volume = lax.map(one_row, jnp.arange(height, dtype=jnp.int32))
    padded = jnp.pad(volume, ((1, 1), (1, 1), (0, 0)))
    weights = agg_weight.astype(jnp.float32)

    def aggregate(index):
        strip = lax.dynamic_slice(padded, (index, jnp.int32(0), jnp.int32(0)), (3, width + 2, DISP)).astype(jnp.float32)
        total = jnp.zeros((width, AGG), jnp.float32)
        for above in range(3):
            for beside in range(3):
                total = total + jnp.dot(strip[above, beside:beside + width], weights[above, beside], precision=lax.Precision.HIGHEST)
        return (total + agg_bias).astype(jnp.bfloat16)
    return lax.map(aggregate, jnp.arange(height, dtype=jnp.int32))
```

```python
import functools
import math

import jax
import jax.numpy as jnp
from jax import lax
from jax.experimental import pallas as pl
from jax.experimental.pallas import tpu as pltpu
from jax.sharding import PartitionSpec as P

DISP = 256
MESH = pl.DeviceIdType.MESH
BF = jnp.bfloat16
F32 = jnp.float32

TILE = 128
RIGHT = 144
ROWS = 544
LANES_L = 768
LANES = 2560


def dot(a, b):
    return lax.dot_general(a, b, (((1,), (0,)), ((), ())), preferred_element_type=F32)


def dot_t(a, b):
    return lax.dot_general(a, b, (((1,), (1,)), ((), ())), preferred_element_type=F32)


def iota(shape, dim):
    return lax.broadcasted_iota(jnp.int32, shape, dim)


def one_hot(cond):
    return jnp.where(cond, 1.0, 0.0).astype(BF)


def row_permutation():
    n, k = iota((256, 192), 0), iota((256, 192), 1)
    b = (n * 171) >> 11
    rest = n - 12 * b
    c, s = rest >> 2, rest & 3
    y = 4 * b - 10 + s
    return one_hot((y >= 0) & (y < 64) & (k == 64 * c + y))


def build_weights(enc_ref, mix_ref, agg_ref, wenc, wmix, wagg):
    row, col = iota((512, 192), 0), iota((512, 192), 1)
    n = row & 63
    j = 2 * (row >> 7) + ((row >> 6) & 1)
    b = (n * 43) >> 9
    rest = n - 12 * b
    base = 64 * (rest >> 2) + 8 * (rest & 3) + j
    for k in range(4):
        a = b - k
        good = (a >= 0) & (a <= 1) & (n < 60) & (col == base + 32 * a)
        part = dot(one_hot(good), enc_ref[...]).astype(BF)
        wenc[0, :, k * 128 : (k + 1) * 128] = part
        for jp in range(4):
            wenc[1, jp * 128 : jp * 128 + 64, k * 128 : (k + 1) * 128] = part[jp * 128 + 64 : jp * 128 + 128]
            wenc[1, jp * 128 + 64 : jp * 128 + 128, k * 128 : (k + 1) * 128] = part[jp * 128 : jp * 128 + 64]
    for beside in range(3):
        for out in range(2):
            lanes = slice((2 * beside + out) * 128, (2 * beside + out + 1) * 128)
            for a in range(4):
                if 0 <= a - out <= 2:
                    wmix[a * 128 : (a + 1) * 128, lanes] = mix_ref[a - out, beside]
                    wagg[a * 256 : (a + 1) * 256, lanes] = agg_ref[a - out, beside]
                else:
                    wmix[a * 128 : (a + 1) * 128, lanes] = jnp.zeros((128, 128), BF)
                    wagg[a * 256 : (a + 1) * 256, lanes] = jnp.zeros((256, 128), BF)


def build_selectors(sel):
    r, x = iota((512, 384), 0), iota((512, 384), 1)
    jj = r >> 6
    j = jnp.where(jj < 4, 2 * jj, 2 * jj - 7)
    q = r & 63
    sel[0] = one_hot(x == 90 + 4 * q + j)
    sel[1] = one_hot(x == 258 - 4 * q + j)


BLOCKS = (
    [(0, 64 * g, 64, 256 * g, 384, 0) for g in range(2)]
    + [(0, 128, 16, 512, 256, 0)]
    + [(1, RIGHT + 64 * g, 64, LANES_L + 1408 - 256 * g, 384, 0) for g in range(6)]
    + [(1, RIGHT + 384, 16, LANES_L, 256, 128)]
)


def gather_taps(even, odd, sel, store):
    for which, row, count, lane, width, skip in BLOCKS:
        lanes, cols = slice(lane, lane + width), slice(skip, skip + width)
        pick = sel[which, :, cols]
        if count != 64:
            pick = pick.reshape(8, 64, width)[:, :count].reshape(8 * count, width)
        half = 4 * count
        te = dot_t(pick[:half], even(lanes))
        to = dot_t(pick[half:], odd(lanes))
        for jp in range(4):
            store(slice(row, row + count), jp, te[jp * count : (jp + 1) * count], to[jp * count : (jp + 1) * count])


def compute_lower(u, wenc, kind, bias, valid, lower, first):
    acc = dot(u[...], wenc[kind])
    for k in range(4):
        part = jnp.maximum(acc[:, k * 128 : (k + 1) * 128] + bias, 0.0)
        lower[:, first + k * 128 : first + (k + 1) * 128] = jnp.where(valid, part, 0.0).astype(BF)


def kernel(
    img, enc_ref, encb_ref, mix_ref, mixb_ref, agg_ref, aggb_ref, out_ref,
    nat, perm, halo, edge, sel, wenc, wmix, wagg, u, lower, zs, feats, volume, stage,
    zsend, zrecv, rsend, rrecv, osend, orecv, own_sem,
):
    r, m = lax.axis_index("rows"), lax.axis_index("cols")
    nr, nz = lax.axis_size("rows"), lax.axis_size("cols")
    t = lax.rem(m + 1, nz)

    def zdev(d):
        return {"cols": lax.rem(m + d + nz, nz)}

    below, above = {"rows": lax.rem(r + 1, nr)}, {"rows": lax.rem(r + nr - 1, nr)}

    barrier = pltpu.get_barrier_semaphore()
    for d in range(1, 16):
        pl.semaphore_signal(barrier, inc=1, device_id=zdev(d), device_id_type=MESH)
    pl.semaphore_signal(barrier, inc=1, device_id=below, device_id_type=MESH)
    pl.semaphore_signal(barrier, inc=1, device_id=above, device_id_type=MESH)
    pl.semaphore_wait(barrier, 17)

    moves = [
        (img.at[1], slice(LANES_L + 1152, LANES_L + 1664), -1),
        (img.at[0], slice(128, 640), -1),
        (img.at[1], slice(LANES_L + 128, LANES_L + 640), 1),
        (img.at[0, :, 0:128], slice(640, 768), -2),
        (img.at[1, :, 0:128], slice(LANES_L + 1664, LANES_L + 1792), -2),
        (img.at[1, :, 384:512], slice(LANES_L, LANES_L + 128), 2),
    ]
    zcopies = [
        pltpu.make_async_remote_copy(
            src_ref=src, dst_ref=nat.at[:, lanes], send_sem=zsend.at[i], recv_sem=zrecv.at[i],
            device_id=zdev(d), device_id_type=MESH,
        )
        for i, (src, lanes, d) in enumerate(moves)
    ]
    for copy in zcopies:
        copy.start()

    build_weights(enc_ref, mix_ref, agg_ref, wenc, wmix, wagg)
    build_selectors(sel)
    shuffle = row_permutation()
    nat[:, 0:128] = img[0, :, 384:512]
    nat[:, LANES_L + 640 : LANES_L + 1152] = img[1]
    feats[RIGHT + 384 :, :] = jnp.zeros((128, 2304), BF)

    row128 = iota((ROWS, 128), 0)
    col_of = jnp.where(row128 < RIGHT, TILE * t - 9 + row128, TILE * t + 129 + RIGHT - row128)
    valid = (col_of >= 0) & (col_of < 2048)

    for copy in zcopies:
        copy.wait()

    def clear(lo, hi):
        nat[:, lo:hi] = jnp.zeros((192, hi - lo), BF)

    @pl.when(t == 0)
    def _():
        clear(0, 128)
        clear(LANES_L, LANES_L + 1152)

    @pl.when(t == 1)
    def _():
        clear(LANES_L, LANES_L + 640)

    @pl.when(t == 2)
    def _():
        clear(LANES_L, LANES_L + 128)

    @pl.when(t == nz - 1)
    def _():
        clear(640, 768)
        clear(LANES_L + 1664, LANES_L + 1792)

    for lo in range(0, LANES, 512):
        perm[:, lo : lo + 512] = dot(shuffle, nat[:, lo : lo + 512]).astype(BF)

    rcopies = [
        pltpu.make_async_remote_copy(
            src_ref=perm.at[lo : lo + 48], dst_ref=halo.at[i], send_sem=rsend.at[i], recv_sem=rrecv.at[i],
            device_id=to, device_id_type=MESH,
        )
        for i, (lo, to) in enumerate(((192, below), (16, above)))
    ]
    for copy in rcopies:
        copy.start()

    low = iota((1, 128), 1) < 64
    enc_bias = encb_ref[...]

    def store_mid(rows, jp, te, to):
        lanes = slice(jp * 128, (jp + 1) * 128)
        e, o = te[:, :128], to[:, :128]
        u[0, rows, lanes] = jnp.where(low, e, o).astype(BF)
        u[1, rows, lanes] = jnp.where(low, o, e).astype(BF)
        u[2, rows, lanes] = jnp.where(low, te[:, 128:], to[:, 128:]).astype(BF)

    def window(w):
        return slice(48 * w, 48 * w + 64)

    gather_taps(
        lambda lanes: jnp.concatenate([perm[window(w), lanes] for w in (1, 2, 3, 3)], axis=0),
        lambda lanes: jnp.concatenate([perm[window(w), lanes] for w in (2, 1, 3, 3)], axis=0),
        sel, store_mid,
    )
    compute_lower(u.at[0], wenc, 0, enc_bias, valid, lower, 512)
    compute_lower(u.at[1], wenc, 1, enc_bias, valid, lower, 1024)
    compute_lower(u.at[2], wenc, 0, enc_bias, valid, lower, 1536)

    for copy in rcopies:
        copy.wait()

    @pl.when(r == 0)
    def _():
        halo[0] = jnp.zeros((48, LANES), BF)

    @pl.when(r == nr - 1)
    def _():
        halo[1] = jnp.zeros((48, LANES), BF)

    edge[0:48] = perm[0:48] + halo[0]
    edge[48:64] = perm[48:64]
    edge[64:80] = perm[192:208]
    edge[80:128] = perm[208:256] + halo[1]

    def store_edge(rows, jp, te, to):
        lanes = slice(jp * 128, (jp + 1) * 128)
        u[0, rows, lanes] = jnp.where(low, te, to).astype(BF)
        u[1, rows, lanes] = jnp.where(low, to, te).astype(BF)

    gather_taps(
        lambda lanes: edge[:, lanes],
        lambda lanes: jnp.concatenate([edge[64:128, lanes], edge[0:64, lanes]], axis=0),
        sel, store_edge,
    )
    compute_lower(u.at[0], wenc, 0, enc_bias, valid, lower, 0)
    compute_lower(u.at[1], wenc, 1, enc_bias, valid, lower, 2048)

    @pl.when(r == 0)
    def _():
        lower[:, 0:256] = jnp.zeros((ROWS, 256), BF)

    @pl.when(r == nr - 1)
    def _():
        lower[:, 2304:2560] = jnp.zeros((ROWS, 256), BF)

    mix_bias = mixb_ref[...]
    rl = iota((RIGHT, 128), 0)
    ql = TILE * t - 8 + rl
    valid_l = (ql >= 0) & (ql < 2048)
    rr = iota((392, 128), 0)
    qr = TILE * t + 128 - rr
    valid_r = (qr >= 0) & (qr < 2048)

    def mix(s, carry):
        lanes = pl.ds(pl.multiple_of(s * 256, 256), 512)
        x = lower[:, lanes]
        z = dot(x, wmix[...])
        zs[:, 0:256] = z[:, 0:256]
        zs[:, 256:512] = z[:, 256:512] + x[:, 128:384].astype(F32)
        zs[:, 512:768] = z[:, 512:768]
        for k in range(2):
            a, b, c = (slice(i * 256 + k * 128, i * 256 + (k + 1) * 128) for i in range(3))
            dst = pl.ds(pl.multiple_of(s * 256 + k * 128, 128), 128)
            fl = zs[0:144, a] + zs[1:145, b] + zs[2:146, c] + mix_bias
            feats[0:144, dst] = jnp.where(valid_l, fl, 0.0).astype(BF)
            o = RIGHT
            fr = zs[o + 2 : o + 394, a] + zs[o + 1 : o + 393, b] + zs[o : o + 392, c] + mix_bias
            feats[o : o + 392, dst] = jnp.where(valid_r, fr, 0.0).astype(BF)
        return carry

    lax.fori_loop(0, 9, mix, 0)

    @pl.when(r == 0)
    def _():
        feats[0:RIGHT, 0:128] = jnp.zeros((RIGHT, 128), BF)

    @pl.when(r == nr - 1)
    def _():
        feats[0:RIGHT, 2176:2304] = jnp.zeros((RIGHT, 128), BF)

    def correlate(n, carry):
        lanes = pl.ds(pl.multiple_of(n * 128, 128), 128)
        scores = dot_t(feats[0:RIGHT, lanes], feats[RIGHT : RIGHT + 512, lanes])
        turned = jnp.concatenate(
            [
                pltpu.roll(scores[lo:hi], 376 + lo, 1, stride=1, stride_axis=0)[:, :DISP]
                for lo, hi in ((0, 64), (64, 128), (128, 144))
            ],
            axis=0,
        )
        dst = pl.ds(pl.multiple_of(n * DISP, DISP), DISP)
        volume[:, dst] = (turned * (1.0 / math.sqrt(128.0))).astype(BF)
        return carry

    lax.fori_loop(0, 18, correlate, 0)

    agg_bias = aggb_ref[...]
    place = pl.ds(pl.multiple_of(t * TILE, TILE), TILE)

    def send(p):
        return pltpu.make_async_remote_copy(
            src_ref=stage.at[p], dst_ref=out_ref.at[0, place], send_sem=osend.at[p], recv_sem=orecv.at[m],
            device_id={"cols": p}, device_id_type=MESH,
        )

    def aggregate(i, carry):
        s = lax.rem(i + lax.div(m, 2) + 1, 8)
        lanes = pl.ds(pl.multiple_of(s * 512, 512), 1024)
        z = dot(volume[:, lanes], wagg[...])
        zs[0:RIGHT] = z
        for k in range(2):
            a, b, c = (slice(i_ * 256 + k * 128, i_ * 256 + (k + 1) * 128) for i_ in range(3))
            stage[2 * s + k] = (zs[7:135, a] + zs[8:136, b] + zs[9:137, c] + agg_bias).astype(BF)
            p = 2 * s + k

            @pl.when(p != m)
            def _():
                send(p).start()

        return carry

    lax.fori_loop(0, 8, aggregate, 0)

    keep = pltpu.make_async_copy(stage.at[m], out_ref.at[0, place], own_sem)
    keep.start()
    keep.wait()

    def finish(p, carry):
        @pl.when(p != m)
        def _():
            send(p).wait_send()
            src = pl.ds(pl.multiple_of(lax.rem(p + 1, nz) * TILE, TILE), TILE)
            pltpu.make_async_remote_copy(
                src_ref=stage.at[p], dst_ref=out_ref.at[0, src], send_sem=osend.at[p], recv_sem=orecv.at[p],
                device_id={"cols": p}, device_id_type=MESH,
            ).wait_recv()

        return carry

    lax.fori_loop(0, 16, finish, 0)


def local(images, enc_weight, enc_bias, mix_weight, mix_bias, agg_weight, agg_bias):
    vmem = pl.BlockSpec(memory_space=pltpu.VMEM)
    return pl.pallas_call(
        kernel,
        out_shape=jax.ShapeDtypeStruct((1, 2048, 128), BF),
        in_specs=[vmem] * 7,
        out_specs=vmem,
        scratch_shapes=[
            pltpu.VMEM((192, LANES), BF),
            pltpu.VMEM((256, LANES), BF),
            pltpu.VMEM((2, 48, LANES), BF),
            pltpu.VMEM((128, LANES), BF),
            pltpu.VMEM((2, 512, 384), BF),
            pltpu.VMEM((2, 512, 512), BF),
            pltpu.VMEM((512, 768), BF),
            pltpu.VMEM((1024, 768), BF),
            pltpu.VMEM((3, ROWS, 512), BF),
            pltpu.VMEM((ROWS, 2560), BF),
            pltpu.VMEM((ROWS, 768), F32),
            pltpu.VMEM((RIGHT + 512, 2304), BF),
            pltpu.VMEM((RIGHT, 18 * DISP), BF),
            pltpu.VMEM((16, 128, 128), BF),
            pltpu.SemaphoreType.DMA((6,)),
            pltpu.SemaphoreType.DMA((6,)),
            pltpu.SemaphoreType.DMA((2,)),
            pltpu.SemaphoreType.DMA((2,)),
            pltpu.SemaphoreType.DMA((16,)),
            pltpu.SemaphoreType.DMA((16,)),
            pltpu.SemaphoreType.DMA,
        ],
        compiler_params=pltpu.CompilerParams(
            collective_id=0, has_side_effects=True, vmem_limit_bytes=48 * 1024 * 1024
        ),
        name="stereo",
    )(
        images.reshape(2, 192, 512),
        enc_weight.reshape(192, 128),
        enc_bias.reshape(1, 128),
        mix_weight,
        mix_bias.reshape(1, 128),
        agg_weight,
        agg_bias.reshape(1, 128),
    )


def solution(mesh):
    return jax.shard_map(
        local,
        mesh=mesh,
        in_specs=(P(None, None, "rows", "cols"), P(), P(), P(), P(), P(), P()),
        out_specs=P(("rows", "cols"), None, None),
        check_vma=False,
    )
```

```python
import math

import jax
import jax.numpy as jnp
from jax import lax
from jax.experimental import pallas as pl
from jax.experimental.pallas import tpu as pltpu
from jax.sharding import PartitionSpec as P

DISP = 256
MESH = pl.DeviceIdType.MESH
BF = jnp.bfloat16
F32 = jnp.float32

TILE = 128
RIGHT = 144
ROWS = 544
LANES_L = 768
LANES = 2560


def dot(a, b):
    return lax.dot_general(a, b, (((1,), (0,)), ((), ())), preferred_element_type=F32)


def dot_t(a, b):
    return lax.dot_general(a, b, (((1,), (1,)), ((), ())), preferred_element_type=F32)


def iota(shape, dim):
    return lax.broadcasted_iota(jnp.int32, shape, dim)


def one_hot(cond):
    return jnp.where(cond, 1.0, 0.0).astype(BF)


def row_permutation():
    n, k = iota((64, 96), 0), iota((64, 96), 1)
    b = (n * 43) >> 9
    rest = n - 12 * b
    return one_hot((n < 60) & (k == 32 * (rest >> 2) + 4 * b + (rest & 3) + 6))


def build_weights(enc_ref, mix_ref, agg_ref, wenc, wmix, wagg):
    row, col = iota((512, 192), 0), iota((512, 192), 1)
    n = row & 63
    j = 2 * (row >> 7) + ((row >> 6) & 1)
    b = (n * 43) >> 9
    rest = n - 12 * b
    base = 64 * (rest >> 2) + 8 * (rest & 3) + j
    for k in range(4):
        a = b - k
        good = (a >= 0) & (a <= 1) & (n < 60) & (col == base + 32 * a)
        part = dot(one_hot(good), enc_ref[...]).astype(BF)
        wenc[0, :, k * 128 : (k + 1) * 128] = part
        for jp in range(4):
            wenc[1, jp * 128 : jp * 128 + 64, k * 128 : (k + 1) * 128] = part[jp * 128 + 64 : jp * 128 + 128]
            wenc[1, jp * 128 + 64 : jp * 128 + 128, k * 128 : (k + 1) * 128] = part[jp * 128 : jp * 128 + 64]
    for beside in range(3):
        for out in range(2):
            lanes = slice((2 * beside + out) * 128, (2 * beside + out + 1) * 128)
            for a in range(4):
                if 0 <= a - out <= 2:
                    wmix[a * 128 : (a + 1) * 128, lanes] = mix_ref[a - out, beside]
                    wagg[a * 256 : (a + 1) * 256, lanes] = agg_ref[a - out, beside]
                else:
                    wmix[a * 128 : (a + 1) * 128, lanes] = jnp.zeros((128, 128), BF)
                    wagg[a * 256 : (a + 1) * 256, lanes] = jnp.zeros((256, 128), BF)


def build_selectors(sel):
    r, x = iota((512, 384), 0), iota((512, 384), 1)
    jj = r >> 6
    j = jnp.where(jj < 4, 2 * jj, 2 * jj - 7)
    q = r & 63
    sel[0] = one_hot(x == 90 + 4 * q + j)
    sel[1] = one_hot(x == 258 - 4 * q + j)


BLOCKS = (
    [(0, 64 * g, 64, 256 * g, 384, 0) for g in range(2)]
    + [(0, 128, 16, 512, 256, 0)]
    + [(1, RIGHT + 64 * g, 64, LANES_L + 1408 - 256 * g, 384, 0) for g in range(6)]
    + [(1, RIGHT + 384, 16, LANES_L, 256, 128)]
)


def gather_taps(even, odd, sel, store):
    for which, row, count, lane, width, skip in BLOCKS:
        lanes, cols = slice(lane, lane + width), slice(skip, skip + width)
        pick = sel[which, :, cols]
        if count != 64:
            pick = pick.reshape(8, 64, width)[:, :count].reshape(8 * count, width)
        half = 4 * count
        te = dot_t(pick[:half], even(lanes))
        to = dot_t(pick[half:], odd(lanes))
        for jp in range(4):
            store(slice(row, row + count), jp, te[jp * count : (jp + 1) * count], to[jp * count : (jp + 1) * count])


def compute_lower(u, weights, bias, valid, lower, first):
    acc = dot(u[...], weights[...])
    for k in range(4):
        part = jnp.maximum(acc[:, k * 128 : (k + 1) * 128] + bias, 0.0)
        lanes = pl.ds(pl.multiple_of(first + k * 128, 128), 128)
        lower[:, lanes] = jnp.where(valid, part, 0.0).astype(BF)


def kernel(
    img, enc_hbm, encb_ref, mix_hbm, mixb_ref, agg_hbm, aggb_ref, out_ref,
    margin, enc_ref, mix_ref, agg_ref, nat, thin, strips, taken, sel, wenc, wmix, wagg,
    u, lower, zs, feats, volume, stage,
    in_sem, zsend, zrecv, rsend, rrecv, osend, orecv, own_sem, near_sem, far_sem,
):
    r, m = lax.axis_index("rows"), lax.axis_index("cols")
    nr, nz = lax.axis_size("rows"), lax.axis_size("cols")
    t = lax.rem(m + 1, nz)

    def zdev(d):
        return {"cols": lax.rem(m + d + nz, nz)}

    below, above = {"rows": lax.rem(r + 1, nr)}, {"rows": lax.rem(r + nr - 1, nr)}

    def signal(sem, device):
        pl.semaphore_signal(sem, inc=1, device_id=device, device_id_type=MESH)

    inner = slice(16, 80)
    ours = slice(LANES_L + 640, LANES_L + 1152)
    loads = [
        pltpu.make_async_copy(src, dst, in_sem.at[i])
        for i, (src, dst) in enumerate(
            (
                (img.at[0, :, :, 0:128], margin),
                (img.at[1], nat.at[:, inner, ours]),
                (img.at[0, :, :, 384:512], nat.at[:, inner, 0:128]),
                (enc_hbm, enc_ref),
                (mix_hbm, mix_ref),
                (agg_hbm, agg_ref),
            )
        )
    ]
    for load in loads:
        load.start()

    barrier = pltpu.get_barrier_semaphore()
    for device in (zdev(1), zdev(-1), zdev(2), zdev(-2), below, above):
        signal(barrier, device)
    pl.semaphore_wait(barrier, 6)

    def zcopy(i, src, dst, d):
        return pltpu.make_async_remote_copy(
            src_ref=src, dst_ref=dst, send_sem=zsend.at[i], recv_sem=zrecv.at[i],
            device_id=zdev(d), device_id_type=MESH,
        )

    moves = ((0, 128, -1), (1, LANES_L + 1152, -1), (1, LANES_L + 128, 1))

    def tiles(part, lo, hi):
        return [
            zcopy(3 * part + i, img.at[n, :, lo:hi], nat.at[:, 16 + lo : 16 + hi, lane : lane + 512], d)
            for i, (n, lane, d) in enumerate(moves)
        ]

    upper, rest = tiles(0, 0, 48), tiles(1, 48, 64)
    for copy in upper + rest:
        copy.start()
    signal(near_sem, zdev(2))
    signal(near_sem, zdev(-2))

    for load in loads[0:3]:
        load.wait()
    pick = iota((16, 128), 1) - iota((16, 128), 0)
    first, last = one_hot(pick == 0), one_hot(pick == 112)
    o = LANES_L + 640
    thin[0, :, 0:192] = dot_t(first, margin[...].reshape(192, 128)).astype(BF)
    thin[1, :, 0:192] = dot_t(first, nat[:, inner, o : o + 128].reshape(192, 128)).astype(BF)
    thin[2, :, 0:192] = dot_t(last, nat[:, inner, o + 384 : o + 512].reshape(192, 128)).astype(BF)
    edges = [
        zcopy(6, thin.at[0], strips.at[0, 0:16], -2),
        zcopy(7, thin.at[1], strips.at[1, 0:16], -2),
        zcopy(8, thin.at[2], strips.at[2, 112:128], 2),
    ]
    for copy in edges:
        copy.start()

    strips[0, 16:128] = jnp.zeros((112, 256), BF)
    strips[1, 16:128] = jnp.zeros((112, 256), BF)
    strips[2, 0:112] = jnp.zeros((112, 256), BF)
    build_selectors(sel)
    shuffle = row_permutation()
    for load in loads[3:]:
        load.wait()
    build_weights(enc_ref, mix_ref, agg_ref, wenc, wmix, wagg)
    feats[RIGHT + 384 :, :] = jnp.zeros((128, 2304), BF)

    row128 = iota((ROWS, 128), 0)
    col_of = jnp.where(row128 < RIGHT, TILE * t - 9 + row128, TILE * t + 129 + RIGHT - row128)
    valid = (col_of >= 0) & (col_of < 2048)

    def clear(rows, lo, hi):
        nat[:, rows, lo:hi] = jnp.zeros((3, rows.stop - rows.start, hi - lo), BF)

    pl.semaphore_wait(near_sem, 2)
    signal(far_sem, zdev(4))
    signal(far_sem, zdev(-4))

    for copy in edges:
        copy.wait()
    same = one_hot(iota((192, 192), 0) == iota((192, 192), 1))
    for i, lane in ((0, 640), (1, LANES_L + 1664), (2, LANES_L)):
        strip = dot_t(same, strips[i, :, 0:192]).astype(BF)
        nat[:, inner, lane : lane + 128] = strip.reshape(3, 64, 128)

    @pl.when(t == 0)
    def _():
        clear(inner, 0, 128)
        clear(inner, LANES_L, LANES_L + 128)
        clear(inner, LANES_L + 640, LANES_L + 1152)

    @pl.when((t == 1) | (t == 2))
    def _():
        clear(inner, LANES_L, LANES_L + 128)

    @pl.when(t == nz - 1)
    def _():
        clear(inner, 640, 768)
        clear(inner, LANES_L + 1664, LANES_L + 1792)

    def arrived(copies, rows):
        for copy in copies:
            copy.wait()

        @pl.when((t == 0) | (t == 1))
        def _():
            clear(rows, LANES_L + 128, LANES_L + 640)

    def rcopy(i, lo, to, device):
        return pltpu.make_async_remote_copy(
            src_ref=nat.at[:, lo : lo + 16], dst_ref=nat.at[:, to : to + 16], send_sem=rsend.at[i], recv_sem=rrecv.at[i],
            device_id=device, device_id_type=MESH,
        )

    up, down = rcopy(0, 16, 80, above), rcopy(1, 64, 0, below)

    arrived(upper, slice(16, 64))
    up.start()

    low = iota((1, 128), 1) < 64
    enc_bias = encb_ref[...]

    def take(w):
        for lo in range(0, LANES, 512):
            x = nat[:, 16 * w : 16 * w + 32, lo : lo + 512].reshape(96, 512)
            taken[w, :, lo : lo + 512] = dot(shuffle, x).astype(BF)

    def joined(order):
        return lambda lanes: jnp.concatenate([taken[w, :, lanes] for w in order], axis=0)

    def store_mid(rows, jp, te, to):
        lanes = slice(jp * 128, (jp + 1) * 128)
        u[1, rows, lanes] = jnp.where(low, te, to).astype(BF)
        u[2, rows, lanes] = jnp.where(low, to, te).astype(BF)

    def store_rest(rows, jp, te, to):
        lanes = slice(jp * 128, (jp + 1) * 128)
        e, o = te[:, :128], to[:, :128]
        u[0, rows, lanes] = jnp.where(low, e, o).astype(BF)
        u[3, rows, lanes] = jnp.where(low, o, e).astype(BF)
        u[4, rows, lanes] = jnp.where(low, te[:, 128:], to[:, 128:]).astype(BF)

    take(1)
    take(2)
    gather_taps(joined((1, 2)), joined((2, 1)), sel, store_mid)
    arrived(rest, slice(64, 80))
    down.start()
    pl.semaphore_wait(far_sem, 2)

    def gather_rest():
        up.wait()
        down.wait()

        @pl.when(r == 0)
        def _():
            clear(slice(0, 16), 0, LANES)

        @pl.when(r == nr - 1)
        def _():
            clear(slice(80, 96), 0, LANES)

        for w in (0, 3, 4):
            take(w)
        gather_taps(joined((0, 3, 4, 4)), joined((3, 0, 4, 4)), sel, store_rest)

    mix_bias = mixb_ref[...]
    ql = TILE * t - 8 + iota((RIGHT, 128), 0)
    valid_l = (ql >= 0) & (ql < 2048)
    qr = TILE * t + 128 - iota((392, 128), 0)
    valid_r = (qr >= 0) & (qr < 2048)

    def mix(s):
        lanes = pl.ds(pl.multiple_of(s * 256, 256), 512)
        x = lower[:, lanes]
        z = dot(x, wmix[...])
        zs[:, 0:256] = z[:, 0:256]
        zs[:, 256:512] = z[:, 256:512] + x[:, 128:384].astype(F32)
        zs[:, 512:768] = z[:, 512:768]
        for k in range(2):
            a, b, c = (slice(i * 256 + k * 128, i * 256 + (k + 1) * 128) for i in range(3))
            dst = pl.ds(pl.multiple_of(s * 256 + k * 128, 128), 128)
            fl = zs[0:144, a] + zs[1:145, b] + zs[2:146, c] + mix_bias
            feats[0:144, dst] = jnp.where(valid_l, fl, 0.0).astype(BF)
            o = RIGHT
            fr = zs[o + 2 : o + 394, a] + zs[o + 1 : o + 393, b] + zs[o : o + 392, c] + mix_bias
            feats[o : o + 392, dst] = jnp.where(valid_r, fr, 0.0).astype(BF)

        @pl.when((r == 0) & (s == 0))
        def _():
            feats[0:RIGHT, 0:128] = jnp.zeros((RIGHT, 128), BF)

        @pl.when((r == nr - 1) & (s == 8))
        def _():
            feats[0:RIGHT, 2176:2304] = jnp.zeros((RIGHT, 128), BF)

    def correlate(n):
        lanes = pl.ds(pl.multiple_of(n * 128, 128), 128)
        scores = dot_t(feats[0:RIGHT, lanes], feats[RIGHT : RIGHT + 512, lanes])
        turned = jnp.concatenate(
            [
                pltpu.roll(scores[lo:hi], 376 + lo, 1, stride=1, stride_axis=0)[:, :DISP]
                for lo, hi in ((0, 64), (64, 128), (128, 144))
            ],
            axis=0,
        )
        dst = pl.ds(pl.multiple_of(n * DISP, DISP), DISP)
        volume[:, dst] = (turned * (1.0 / math.sqrt(128.0))).astype(BF)

    agg_bias = aggb_ref[...]
    place = pl.ds(pl.multiple_of(t * TILE, TILE), TILE)

    def send(p):
        return pltpu.make_async_remote_copy(
            src_ref=stage.at[p], dst_ref=out_ref.at[0, place], send_sem=osend.at[p], recv_sem=orecv.at[m],
            device_id={"cols": p}, device_id_type=MESH,
        )

    def aggregate(s):
        lanes = pl.ds(pl.multiple_of(s * 512, 512), 1024)
        zs[0:RIGHT] = dot(volume[:, lanes], wagg[...])
        for k in range(2):
            a, b, c = (slice(i * 256 + k * 128, i * 256 + (k + 1) * 128) for i in range(3))
            p = 2 * s + k
            stage[p] = (zs[7:135, a] + zs[8:136, b] + zs[9:137, c] + agg_bias).astype(BF)

            @pl.when(p != m)
            def _():
                send(p).start()

    def step(i, carry):
        s = jnp.where(i < 5, 4 - i, i)

        @pl.when(i == 3)
        def _():
            gather_rest()

        @pl.when((i == 0) | (lax.rem(i, 2) == 1))
        def _():
            w = jnp.where(i == 0, 2, jnp.where(i < 5, lax.div(3 - i, 2), lax.div(i + 1, 2)))
            kind = jnp.where((w == 2) | (w == 3), 1, 0)
            compute_lower(u.at[w], wenc.at[kind], enc_bias, valid, lower, 512 * w)

            @pl.when((r == 0) & (w == 0))
            def _():
                lower[:, 0:256] = jnp.zeros((ROWS, 256), BF)

            @pl.when((r == nr - 1) & (w == 4))
            def _():
                lower[:, 2304:2560] = jnp.zeros((ROWS, 256), BF)

        mix(s)
        correlate(2 * s)
        correlate(2 * s + 1)

        @pl.when(i > 0)
        def _():
            aggregate(jnp.where(i < 5, s, s - 1))

        return carry

    lax.fori_loop(0, 9, step, 0)

    keep = pltpu.make_async_copy(stage.at[m], out_ref.at[0, place], own_sem)
    keep.start()
    keep.wait()

    def finish(p, carry):
        @pl.when(p != m)
        def _():
            send(p).wait_send()
            src = pl.ds(pl.multiple_of(lax.rem(p + 1, nz) * TILE, TILE), TILE)
            pltpu.make_async_remote_copy(
                src_ref=stage.at[p], dst_ref=out_ref.at[0, src], send_sem=osend.at[p], recv_sem=orecv.at[p],
                device_id={"cols": p}, device_id_type=MESH,
            ).wait_recv()

        return carry

    lax.fori_loop(0, 16, finish, 0)


def local(images, enc_weight, enc_bias, mix_weight, mix_bias, agg_weight, agg_bias):
    vmem, hbm = pl.BlockSpec(memory_space=pltpu.VMEM), pl.BlockSpec(memory_space=pltpu.HBM)
    return pl.pallas_call(
        kernel,
        out_shape=jax.ShapeDtypeStruct((1, 2048, 128), BF),
        in_specs=[hbm, hbm, vmem, hbm, vmem, hbm, vmem],
        out_specs=vmem,
        scratch_shapes=[
            pltpu.VMEM((3, 64, 128), BF),
            pltpu.VMEM((192, 128), BF),
            pltpu.VMEM((3, 3, 128, 128), BF),
            pltpu.VMEM((3, 3, 256, 128), BF),
            pltpu.VMEM((3, 96, LANES), BF),
            pltpu.VMEM((3, 16, 256), BF),
            pltpu.VMEM((3, 128, 256), BF),
            pltpu.VMEM((5, 64, LANES), BF),
            pltpu.VMEM((2, 512, 384), BF),
            pltpu.VMEM((2, 512, 512), BF),
            pltpu.VMEM((512, 768), BF),
            pltpu.VMEM((1024, 768), BF),
            pltpu.VMEM((5, ROWS, 512), BF),
            pltpu.VMEM((ROWS, 2560), BF),
            pltpu.VMEM((ROWS, 768), F32),
            pltpu.VMEM((RIGHT + 512, 2304), BF),
            pltpu.VMEM((RIGHT, 18 * DISP), BF),
            pltpu.VMEM((16, 128, 128), BF),
            pltpu.SemaphoreType.DMA((6,)),
            pltpu.SemaphoreType.DMA((9,)),
            pltpu.SemaphoreType.DMA((9,)),
            pltpu.SemaphoreType.DMA((2,)),
            pltpu.SemaphoreType.DMA((2,)),
            pltpu.SemaphoreType.DMA((16,)),
            pltpu.SemaphoreType.DMA((16,)),
            pltpu.SemaphoreType.DMA,
            pltpu.SemaphoreType.REGULAR,
            pltpu.SemaphoreType.REGULAR,
        ],
        compiler_params=pltpu.CompilerParams(
            collective_id=0, has_side_effects=True, vmem_limit_bytes=60 * 1024 * 1024
        ),
        name="stereo",
    )(
        images,
        enc_weight.reshape(192, 128),
        enc_bias.reshape(1, 128),
        mix_weight,
        mix_bias.reshape(1, 128),
        agg_weight,
        agg_bias.reshape(1, 128),
    )


def solution(mesh):
    return jax.shard_map(
        local,
        mesh=mesh,
        in_specs=(P(None, None, "rows", "cols"), P(), P(), P(), P(), P(), P()),
        out_specs=P(("rows", "cols"), None, None),
        check_vma=False,
    )
```

```python
import math

import jax
import jax.numpy as jnp
from jax import lax
from jax.experimental import pallas as pl
from jax.experimental.pallas import tpu as pltpu
from jax.sharding import PartitionSpec as P

DISP = 256
MESH = pl.DeviceIdType.MESH
BF = jnp.bfloat16
F32 = jnp.float32

TILE = 128
RIGHT = 144
ROWS = 544
LANES_L = 768
LANES = 2560


def dot(a, b):
    return lax.dot_general(a, b, (((1,), (0,)), ((), ())), preferred_element_type=F32)


def dot_t(a, b):
    return lax.dot_general(a, b, (((1,), (1,)), ((), ())), preferred_element_type=F32)


def iota(shape, dim):
    return lax.broadcasted_iota(jnp.int32, shape, dim)


def one_hot(cond):
    return jnp.where(cond, 1.0, 0.0).astype(BF)


def row_permutation():
    n, k = iota((64, 96), 0), iota((64, 96), 1)
    b = (n * 43) >> 9
    rest = n - 12 * b
    return one_hot((n < 60) & (k == 32 * (rest >> 2) + 4 * b + (rest & 3) + 6))


def build_weights(enc_ref, mix_ref, agg_ref, wenc, wmix, wagg):
    row, col = iota((512, 192), 0), iota((512, 192), 1)
    n = row & 63
    j = 2 * (row >> 7) + ((row >> 6) & 1)
    b = (n * 43) >> 9
    rest = n - 12 * b
    base = 64 * (rest >> 2) + 8 * (rest & 3) + j
    for k in range(4):
        a = b - k
        good = (a >= 0) & (a <= 1) & (n < 60) & (col == base + 32 * a)
        part = dot(one_hot(good), enc_ref[...]).astype(BF)
        wenc[0, :, k * 128 : (k + 1) * 128] = part
        for jp in range(4):
            wenc[1, jp * 128 : jp * 128 + 64, k * 128 : (k + 1) * 128] = part[jp * 128 + 64 : jp * 128 + 128]
            wenc[1, jp * 128 + 64 : jp * 128 + 128, k * 128 : (k + 1) * 128] = part[jp * 128 : jp * 128 + 64]
    for beside in range(3):
        for out in range(2):
            lanes = slice((2 * beside + out) * 128, (2 * beside + out + 1) * 128)
            for a in range(4):
                if 0 <= a - out <= 2:
                    wmix[a * 128 : (a + 1) * 128, lanes] = mix_ref[a - out, beside]
                    wagg[a * 256 : (a + 1) * 256, lanes] = agg_ref[a - out, beside]
                else:
                    wmix[a * 128 : (a + 1) * 128, lanes] = jnp.zeros((128, 128), BF)
                    wagg[a * 256 : (a + 1) * 256, lanes] = jnp.zeros((256, 128), BF)


def build_selectors(sel):
    r, x = iota((512, 384), 0), iota((512, 384), 1)
    jj = r >> 6
    j = jnp.where(jj < 4, 2 * jj, 2 * jj - 7)
    q = r & 63
    sel[0] = one_hot(x == 90 + 4 * q + j)
    sel[1] = one_hot(x == 258 - 4 * q + j)


BLOCKS = (
    [(0, 64 * g, 64, 256 * g, 384, 0) for g in range(2)]
    + [(0, 128, 16, 512, 256, 0)]
    + [(1, RIGHT + 64 * g, 64, LANES_L + 1408 - 256 * g, 384, 0) for g in range(6)]
    + [(1, RIGHT + 384, 16, LANES_L, 256, 128)]
)


def gather_taps(even, odd, sel, store):
    for which, row, count, lane, width, skip in BLOCKS:
        lanes, cols = slice(lane, lane + width), slice(skip, skip + width)
        pick = sel[which, :, cols]
        if count != 64:
            pick = pick.reshape(8, 64, width)[:, :count].reshape(8 * count, width)
        half = 4 * count
        te = dot_t(pick[:half], even(lanes))
        to = dot_t(pick[half:], odd(lanes))
        for jp in range(4):
            store(slice(row, row + count), jp, te[jp * count : (jp + 1) * count], to[jp * count : (jp + 1) * count])


def compute_lower(u, weights, bias, valid, lower, first):
    acc = dot(u[...], weights[...])
    for k in range(4):
        part = jnp.maximum(acc[:, k * 128 : (k + 1) * 128] + bias, 0.0)
        lanes = pl.ds(pl.multiple_of(first + k * 128, 128), 128)
        lower[:, lanes] = jnp.where(valid, part, 0.0).astype(BF)


def kernel(
    img, enc_hbm, encb_ref, mix_hbm, mixb_ref, agg_hbm, aggb_ref, out_ref,
    margin, enc_ref, mix_ref, agg_ref, nat, thin, strips, taken, sel, wenc, wmix, wagg,
    u, lower, zs, feats, volume, stage,
    in_sem, zsend, zrecv, rsend, rrecv, osend, orecv, own_sem, near_sem, far_sem,
):
    r, m = lax.axis_index("rows"), lax.axis_index("cols")
    nr, nz = lax.axis_size("rows"), lax.axis_size("cols")
    t = lax.rem(m + 1, nz)
    half = lax.div(nz, 2)
    ahead = m < half
    first_w, third_w = jnp.where(ahead, 3, 1), jnp.where(ahead, 1, 3)

    def zdev(d):
        return {"cols": lax.rem(m + d + nz, nz)}

    below, above = {"rows": lax.rem(r + 1, nr)}, {"rows": lax.rem(r + nr - 1, nr)}

    def signal(sem, device):
        pl.semaphore_signal(sem, inc=1, device_id=device, device_id_type=MESH)

    inner = slice(16, 80)
    ours = slice(LANES_L + 640, LANES_L + 1152)
    loads = [
        pltpu.make_async_copy(src, dst, in_sem.at[i])
        for i, (src, dst) in enumerate(
            (
                (img.at[0, :, :, 0:128], margin),
                (img.at[1], nat.at[:, inner, ours]),
                (img.at[0, :, :, 384:512], nat.at[:, inner, 0:128]),
                (enc_hbm, enc_ref),
                (mix_hbm, mix_ref),
                (agg_hbm, agg_ref),
            )
        )
    ]
    for load in loads:
        load.start()

    barrier = pltpu.get_barrier_semaphore()
    for device in (zdev(1), zdev(-1), zdev(2), zdev(-2), below, above):
        signal(barrier, device)
    pl.semaphore_wait(barrier, 6)

    def zcopy(i, src, dst, d):
        return pltpu.make_async_remote_copy(
            src_ref=src, dst_ref=dst, send_sem=zsend.at[i], recv_sem=zrecv.at[i],
            device_id=zdev(d), device_id_type=MESH,
        )

    moves = ((0, 128, -1), (1, LANES_L + 1152, -1), (1, LANES_L + 128, 1))

    def tiles(part, size, low_start, high_start):
        copies = []
        for i, (n, lane, d) in enumerate(moves):
            target = lax.rem(m + d + nz, nz)
            lo = pl.multiple_of(jnp.where(target < half, low_start, high_start), 16)
            dst = nat.at[:, pl.ds(pl.multiple_of(lo + 16, 16), size), lane : lane + 512]
            copies.append(zcopy(3 * part + i, img.at[n, :, pl.ds(lo, size)], dst, d))
        return copies

    middle, second, rest = tiles(0, 32, 16, 16), tiles(1, 16, 48, 0), tiles(2, 16, 0, 48)
    for copy in middle:
        copy.start()
    signal(near_sem, zdev(2))
    signal(near_sem, zdev(-2))

    for load in loads[0:3]:
        load.wait()
    pick = iota((16, 128), 1) - iota((16, 128), 0)
    first, last = one_hot(pick == 0), one_hot(pick == 112)
    o = LANES_L + 640
    thin[0, :, 0:192] = dot_t(first, margin[...].reshape(192, 128)).astype(BF)
    thin[1, :, 0:192] = dot_t(first, nat[:, inner, o : o + 128].reshape(192, 128)).astype(BF)
    thin[2, :, 0:192] = dot_t(last, nat[:, inner, o + 384 : o + 512].reshape(192, 128)).astype(BF)
    edges = [
        zcopy(9, thin.at[0], strips.at[0, 0:16], -2),
        zcopy(10, thin.at[1], strips.at[1, 0:16], -2),
        zcopy(11, thin.at[2], strips.at[2, 112:128], 2),
    ]
    for copy in edges + second + rest:
        copy.start()

    strips[0, 16:128] = jnp.zeros((112, 256), BF)
    strips[1, 16:128] = jnp.zeros((112, 256), BF)
    strips[2, 0:112] = jnp.zeros((112, 256), BF)
    build_selectors(sel)
    shuffle = row_permutation()
    for load in loads[3:]:
        load.wait()
    build_weights(enc_ref, mix_ref, agg_ref, wenc, wmix, wagg)
    feats[RIGHT + 384 :, :] = jnp.zeros((128, 2304), BF)

    row128 = iota((ROWS, 128), 0)
    col_of = jnp.where(row128 < RIGHT, TILE * t - 9 + row128, TILE * t + 129 + RIGHT - row128)
    valid = (col_of >= 0) & (col_of < 2048)

    def clear(rows, lo, hi):
        size = rows.size if isinstance(rows, pl.Slice) else rows.stop - rows.start
        nat[:, rows, lo:hi] = jnp.zeros((3, size, hi - lo), BF)

    pl.semaphore_wait(near_sem, 2)
    signal(far_sem, zdev(4))
    signal(far_sem, zdev(-4))

    for copy in edges:
        copy.wait()
    same = one_hot(iota((192, 192), 0) == iota((192, 192), 1))
    for i, lane in ((0, 640), (1, LANES_L + 1664), (2, LANES_L)):
        strip = dot_t(same, strips[i, :, 0:192]).astype(BF)
        nat[:, inner, lane : lane + 128] = strip.reshape(3, 64, 128)

    @pl.when(t == 0)
    def _():
        clear(inner, 0, 128)
        clear(inner, LANES_L, LANES_L + 128)
        clear(inner, LANES_L + 640, LANES_L + 1152)

    @pl.when((t == 1) | (t == 2))
    def _():
        clear(inner, LANES_L, LANES_L + 128)

    @pl.when(t == nz - 1)
    def _():
        clear(inner, 640, 768)
        clear(inner, LANES_L + 1664, LANES_L + 1792)

    def arrived(copies, rows):
        for copy in copies:
            copy.wait()

        @pl.when((t == 0) | (t == 1))
        def _():
            clear(rows, LANES_L + 128, LANES_L + 640)

    def rcopy(i, down):
        lo, to = pl.multiple_of(jnp.where(down, 64, 16), 16), pl.multiple_of(jnp.where(down, 0, 80), 16)
        return pltpu.make_async_remote_copy(
            src_ref=nat.at[:, pl.ds(lo, 16)], dst_ref=nat.at[:, pl.ds(to, 16)], send_sem=rsend.at[i], recv_sem=rrecv.at[i],
            device_id={"rows": lax.rem(r + jnp.where(down, 1, nr - 1), nr)}, device_id_type=MESH,
        )

    halos = rcopy(0, ahead), rcopy(1, jnp.logical_not(ahead))

    low = iota((1, 128), 1) < 64
    enc_bias = encb_ref[...]

    def take(w):
        for lo in range(0, LANES, 512):
            x = nat[:, pl.ds(pl.multiple_of(16 * w, 16), 32), lo : lo + 512].reshape(96, 512)
            taken[w, :, lo : lo + 512] = dot(shuffle, x).astype(BF)

    def joined(order):
        return lambda lanes: jnp.concatenate([taken[w, :, lanes] for w in order], axis=0)

    def gather_one(w):
        def store_one(rows, jp, te, to):
            u[w, rows, jp * 128 : (jp + 1) * 128] = jnp.where(low, te, to).astype(BF)

        take(w)
        gather_taps(joined((w, w)), joined((w, w)), sel, store_one)

    def store_rest(rows, jp, te, to):
        lanes = slice(jp * 128, (jp + 1) * 128)
        e, o = te[:, :128], to[:, :128]
        u[0, rows, lanes] = jnp.where(low, e, o).astype(BF)
        u[third_w, rows, lanes] = jnp.where(low, o, e).astype(BF)
        u[4, rows, lanes] = jnp.where(low, te[:, 128:], to[:, 128:]).astype(BF)

    arrived(middle, slice(32, 64))

    def gather_first():
        gather_one(2)

    def gather_second():
        arrived(second, pl.ds(pl.multiple_of(jnp.where(ahead, 64, 16), 16), 16))
        halos[0].start()
        gather_one(first_w)
        arrived(rest, pl.ds(pl.multiple_of(jnp.where(ahead, 16, 64), 16), 16))
        halos[1].start()
        pl.semaphore_wait(far_sem, 2)

    def gather_rest():
        for copy in halos:
            copy.wait()

        @pl.when(r == 0)
        def _():
            clear(slice(0, 16), 0, LANES)

        @pl.when(r == nr - 1)
        def _():
            clear(slice(80, 96), 0, LANES)

        for w in (0, third_w, 4):
            take(w)
        gather_taps(joined((0, third_w, 4, 4)), joined((third_w, 0, 4, 4)), sel, store_rest)

    mix_bias = mixb_ref[...]
    ql = TILE * t - 8 + iota((RIGHT, 128), 0)
    valid_l = (ql >= 0) & (ql < 2048)
    qr = TILE * t + 128 - iota((392, 128), 0)
    valid_r = (qr >= 0) & (qr < 2048)

    def mix(s):
        lanes = pl.ds(pl.multiple_of(s * 256, 256), 512)
        x = lower[:, lanes]
        z = dot(x, wmix[...])
        zs[:, 0:256] = z[:, 0:256]
        zs[:, 256:512] = z[:, 256:512] + x[:, 128:384].astype(F32)
        zs[:, 512:768] = z[:, 512:768]
        for k in range(2):
            a, b, c = (slice(i * 256 + k * 128, i * 256 + (k + 1) * 128) for i in range(3))
            dst = pl.ds(pl.multiple_of(s * 256 + k * 128, 128), 128)
            fl = zs[0:144, a] + zs[1:145, b] + zs[2:146, c] + mix_bias
            feats[0:144, dst] = jnp.where(valid_l, fl, 0.0).astype(BF)
            o = RIGHT
            fr = zs[o + 2 : o + 394, a] + zs[o + 1 : o + 393, b] + zs[o : o + 392, c] + mix_bias
            feats[o : o + 392, dst] = jnp.where(valid_r, fr, 0.0).astype(BF)

        @pl.when((r == 0) & (s == 0))
        def _():
            feats[0:RIGHT, 0:128] = jnp.zeros((RIGHT, 128), BF)

        @pl.when((r == nr - 1) & (s == 8))
        def _():
            feats[0:RIGHT, 2176:2304] = jnp.zeros((RIGHT, 128), BF)

    def correlate(n):
        lanes = pl.ds(pl.multiple_of(n * 128, 128), 128)
        scores = dot_t(feats[0:RIGHT, lanes], feats[RIGHT : RIGHT + 512, lanes])
        turned = jnp.concatenate(
            [
                pltpu.roll(scores[lo:hi], 376 + lo, 1, stride=1, stride_axis=0)[:, :DISP]
                for lo, hi in ((0, 64), (64, 128), (128, 144))
            ],
            axis=0,
        )
        dst = pl.ds(pl.multiple_of(n * DISP, DISP), DISP)
        volume[:, dst] = (turned * (1.0 / math.sqrt(128.0))).astype(BF)

    agg_bias = aggb_ref[...]
    place = pl.ds(pl.multiple_of(t * TILE, TILE), TILE)

    def send(p):
        return pltpu.make_async_remote_copy(
            src_ref=stage.at[p], dst_ref=out_ref.at[0, place], send_sem=osend.at[p], recv_sem=orecv.at[m],
            device_id={"cols": p}, device_id_type=MESH,
        )

    def aggregate(s):
        lanes = pl.ds(pl.multiple_of(s * 512, 512), 1024)
        zs[0:RIGHT] = dot(volume[:, lanes], wagg[...])
        for k in range(2):
            a, b, c = (slice(i * 256 + k * 128, i * 256 + (k + 1) * 128) for i in range(3))
            p = 2 * s + k
            stage[p] = (zs[7:135, a] + zs[8:136, b] + zs[9:137, c] + agg_bias).astype(BF)

            @pl.when(p != m)
            def _():
                send(p).start()

    def step(i, carry):
        s = jnp.where(ahead, lax.rem(i + 4, 9), jnp.where(i < 5, 4 - i, i))

        @pl.when(i == 0)
        def _():
            gather_first()

        @pl.when(i == 1)
        def _():
            gather_second()

        @pl.when(i == 3)
        def _():
            gather_rest()

        @pl.when((i == 0) | (i == 1) | (i == 3) | (i == 5) | (i == jnp.where(ahead, 6, 7)))
        def _():
            late = jnp.where(ahead, jnp.where(i == 3, 4, jnp.where(i == 5, 0, 1)), jnp.where(i == 3, 0, jnp.where(i == 5, 3, 4)))
            w = jnp.where(i == 0, 2, jnp.where(i == 1, first_w, late))
            kind = jnp.where(w == third_w, 1, 0)
            compute_lower(u.at[w], wenc.at[kind], enc_bias, valid, lower, 512 * w)

            @pl.when((r == 0) & (w == 0))
            def _():
                lower[:, 0:256] = jnp.zeros((ROWS, 256), BF)

            @pl.when((r == nr - 1) & (w == 4))
            def _():
                lower[:, 2304:2560] = jnp.zeros((ROWS, 256), BF)

        mix(s)
        correlate(2 * s)
        correlate(2 * s + 1)

        below_s = ahead | (i > 4)

        @pl.when((i > 0) & ((s > 0) | jnp.logical_not(below_s)))
        def _():
            aggregate(jnp.where(below_s, s - 1, s))

        return carry

    lax.fori_loop(0, 9, step, 0)

    @pl.when(ahead)
    def _():
        aggregate(3)

    keep = pltpu.make_async_copy(stage.at[m], out_ref.at[0, place], own_sem)
    keep.start()
    keep.wait()

    def finish(p, carry):
        @pl.when(p != m)
        def _():
            send(p).wait_send()
            src = pl.ds(pl.multiple_of(lax.rem(p + 1, nz) * TILE, TILE), TILE)
            pltpu.make_async_remote_copy(
                src_ref=stage.at[p], dst_ref=out_ref.at[0, src], send_sem=osend.at[p], recv_sem=orecv.at[p],
                device_id={"cols": p}, device_id_type=MESH,
            ).wait_recv()

        return carry

    lax.fori_loop(0, 16, finish, 0)


def local(images, enc_weight, enc_bias, mix_weight, mix_bias, agg_weight, agg_bias):
    vmem, hbm = pl.BlockSpec(memory_space=pltpu.VMEM), pl.BlockSpec(memory_space=pltpu.HBM)
    return pl.pallas_call(
        kernel,
        out_shape=jax.ShapeDtypeStruct((1, 2048, 128), BF),
        in_specs=[hbm, hbm, vmem, hbm, vmem, hbm, vmem],
        out_specs=hbm,
        scratch_shapes=[
            pltpu.VMEM((3, 64, 128), BF),
            pltpu.VMEM((192, 128), BF),
            pltpu.VMEM((3, 3, 128, 128), BF),
            pltpu.VMEM((3, 3, 256, 128), BF),
            pltpu.VMEM((3, 96, LANES), BF),
            pltpu.VMEM((3, 16, 256), BF),
            pltpu.VMEM((3, 128, 256), BF),
            pltpu.VMEM((5, 64, LANES), BF),
            pltpu.VMEM((2, 512, 384), BF),
            pltpu.VMEM((2, 512, 512), BF),
            pltpu.VMEM((512, 768), BF),
            pltpu.VMEM((1024, 768), BF),
            pltpu.VMEM((5, ROWS, 512), BF),
            pltpu.VMEM((ROWS, 2560), BF),
            pltpu.VMEM((ROWS, 768), F32),
            pltpu.VMEM((RIGHT + 512, 2304), BF),
            pltpu.VMEM((RIGHT, 18 * DISP), BF),
            pltpu.VMEM((16, 128, 128), BF),
            pltpu.SemaphoreType.DMA((6,)),
            pltpu.SemaphoreType.DMA((12,)),
            pltpu.SemaphoreType.DMA((12,)),
            pltpu.SemaphoreType.DMA((2,)),
            pltpu.SemaphoreType.DMA((2,)),
            pltpu.SemaphoreType.DMA((16,)),
            pltpu.SemaphoreType.DMA((16,)),
            pltpu.SemaphoreType.DMA,
            pltpu.SemaphoreType.REGULAR,
            pltpu.SemaphoreType.REGULAR,
        ],
        compiler_params=pltpu.CompilerParams(
            collective_id=0, has_side_effects=True, vmem_limit_bytes=60 * 1024 * 1024
        ),
        name="stereo",
    )(
        images,
        enc_weight.reshape(192, 128),
        enc_bias.reshape(1, 128),
        mix_weight,
        mix_bias.reshape(1, 128),
        agg_weight,
        agg_bias.reshape(1, 128),
    )


def solution(mesh):
    return jax.shard_map(
        local,
        mesh=mesh,
        in_specs=(P(None, None, "rows", "cols"), P(), P(), P(), P(), P(), P()),
        out_specs=P(("rows", "cols"), None, None),
        check_vma=False,
    )
```

```python
import math

import jax
import jax.numpy as jnp
from jax import lax
from jax.experimental import pallas as pl
from jax.experimental.pallas import tpu as pltpu
from jax.sharding import PartitionSpec as P

DISP = 256
MESH = pl.DeviceIdType.MESH
BF = jnp.bfloat16
F32 = jnp.float32

TILE = 128
RIGHT = 144
ROWS = 544
LANES_L = 768
LANES = 2560


def dot(a, b):
    return lax.dot_general(a, b, (((1,), (0,)), ((), ())), preferred_element_type=F32)


def dot_t(a, b):
    return lax.dot_general(a, b, (((1,), (1,)), ((), ())), preferred_element_type=F32)


def iota(shape, dim):
    return lax.broadcasted_iota(jnp.int32, shape, dim)


def one_hot(cond):
    return jnp.where(cond, 1.0, 0.0).astype(BF)


def row_permutation():
    n, k = iota((64, 96), 0), iota((64, 96), 1)
    b = (n * 43) >> 9
    rest = n - 12 * b
    return one_hot((n < 60) & (k == 32 * (rest >> 2) + 4 * b + (rest & 3) + 6))


def build_weights(enc_ref, mix_ref, agg_ref, wenc, wmix, wagg):
    row, col = iota((512, 192), 0), iota((512, 192), 1)
    n = row & 63
    j = 2 * (row >> 7) + ((row >> 6) & 1)
    b = (n * 43) >> 9
    rest = n - 12 * b
    base = 64 * (rest >> 2) + 8 * (rest & 3) + j
    for k in range(4):
        a = b - k
        good = (a >= 0) & (a <= 1) & (n < 60) & (col == base + 32 * a)
        part = dot(one_hot(good), enc_ref[...]).astype(BF)
        wenc[0, :, k * 128 : (k + 1) * 128] = part
        for jp in range(4):
            wenc[1, jp * 128 : jp * 128 + 64, k * 128 : (k + 1) * 128] = part[jp * 128 + 64 : jp * 128 + 128]
            wenc[1, jp * 128 + 64 : jp * 128 + 128, k * 128 : (k + 1) * 128] = part[jp * 128 : jp * 128 + 64]
    for beside in range(3):
        for out in range(2):
            lanes = slice((2 * beside + out) * 128, (2 * beside + out + 1) * 128)
            for a in range(4):
                if 0 <= a - out <= 2:
                    wmix[a * 128 : (a + 1) * 128, lanes] = mix_ref[a - out, beside]
                    wagg[a * 256 : (a + 1) * 256, lanes] = agg_ref[a - out, beside]
                else:
                    wmix[a * 128 : (a + 1) * 128, lanes] = jnp.zeros((128, 128), BF)
                    wagg[a * 256 : (a + 1) * 256, lanes] = jnp.zeros((256, 128), BF)


def build_selectors(sel):
    r, x = iota((512, 384), 0), iota((512, 384), 1)
    jj = r >> 6
    j = jnp.where(jj < 4, 2 * jj, 2 * jj - 7)
    q = r & 63
    sel[0] = one_hot(x == 90 + 4 * q + j)
    sel[1] = one_hot(x == 258 - 4 * q + j)


BLOCKS = (
    [(0, 64 * g, 64, 256 * g, 384, 0) for g in range(2)]
    + [(0, 128, 16, 512, 256, 0)]
    + [(1, RIGHT + 64 * g, 64, LANES_L + 1408 - 256 * g, 384, 0) for g in range(6)]
    + [(1, RIGHT + 384, 16, LANES_L, 256, 128)]
)


def gather_taps(even, odd, sel, store):
    for which, row, count, lane, width, skip in BLOCKS:
        lanes, cols = slice(lane, lane + width), slice(skip, skip + width)
        pick = sel[which, :, cols]
        if count != 64:
            pick = pick.reshape(8, 64, width)[:, :count].reshape(8 * count, width)
        half = 4 * count
        te = dot_t(pick[:half], even(lanes))
        to = dot_t(pick[half:], odd(lanes))
        for jp in range(4):
            store(slice(row, row + count), jp, te[jp * count : (jp + 1) * count], to[jp * count : (jp + 1) * count])


def compute_lower(u, weights, bias, valid, lower, first):
    acc = dot(u[...], weights[...])
    for k in range(4):
        part = jnp.maximum(acc[:, k * 128 : (k + 1) * 128] + bias, 0.0)
        lanes = pl.ds(pl.multiple_of(first + k * 128, 128), 128)
        lower[:, lanes] = jnp.where(valid, part, 0.0).astype(BF)


def kernel(
    img, enc_hbm, encb_ref, mix_hbm, mixb_ref, agg_hbm, aggb_ref, out_ref,
    margin, enc_ref, mix_ref, agg_ref, nat, thin, strips, taken, sel, wenc, wmix, wagg,
    u, lower, zs, feats, volume, stage,
    in_sem, zsend, zrecv, rsend, rrecv, osend, orecv, own_sem, near_sem, far_sem,
):
    r, m = lax.axis_index("rows"), lax.axis_index("cols")
    nr, nz = lax.axis_size("rows"), lax.axis_size("cols")
    t = lax.rem(m + 1, nz)
    half = lax.div(nz, 2)
    ahead = m < half
    first_w, third_w = jnp.where(ahead, 3, 1), jnp.where(ahead, 1, 3)

    def zdev(d):
        return {"cols": lax.rem(m + d + nz, nz)}

    below, above = {"rows": lax.rem(r + 1, nr)}, {"rows": lax.rem(r + nr - 1, nr)}

    def signal(sem, device):
        pl.semaphore_signal(sem, inc=1, device_id=device, device_id_type=MESH)

    inner = slice(16, 80)
    ours = slice(LANES_L + 640, LANES_L + 1152)
    loads = [
        pltpu.make_async_copy(src, dst, in_sem.at[i])
        for i, (src, dst) in enumerate(
            (
                (img.at[0, :, :, 0:128], margin),
                (img.at[1], nat.at[:, inner, ours]),
                (img.at[0, :, :, 384:512], nat.at[:, inner, 0:128]),
                (enc_hbm, enc_ref),
                (mix_hbm, mix_ref),
                (agg_hbm, agg_ref),
            )
        )
    ]
    for load in loads:
        load.start()

    barrier = pltpu.get_barrier_semaphore()
    for device in (zdev(1), zdev(-1), zdev(2), zdev(-2), below, above):
        signal(barrier, device)
    pl.semaphore_wait(barrier, 6)

    def zcopy(i, src, dst, d):
        return pltpu.make_async_remote_copy(
            src_ref=src, dst_ref=dst, send_sem=zsend.at[i], recv_sem=zrecv.at[i],
            device_id=zdev(d), device_id_type=MESH,
        )

    moves = ((0, 128, -1), (1, LANES_L + 1152, -1), (1, LANES_L + 128, 1))

    def tiles(part, size, low_start, high_start):
        copies = []
        for i, (n, lane, d) in enumerate(moves):
            target = lax.rem(m + d + nz, nz)
            lo = pl.multiple_of(jnp.where(target < half, low_start, high_start), 16)
            dst = nat.at[:, pl.ds(pl.multiple_of(lo + 16, 16), size), lane : lane + 512]
            copies.append(zcopy(3 * part + i, img.at[n, :, pl.ds(lo, size)], dst, d))
        return copies

    middle, second, rest = tiles(0, 32, 16, 16), tiles(1, 16, 48, 0), tiles(2, 16, 0, 48)
    for copy in middle:
        copy.start()
    signal(near_sem, zdev(2))
    signal(near_sem, zdev(-2))

    for load in loads[0:3]:
        load.wait()
    pick = iota((16, 128), 1) - iota((16, 128), 0)
    first, last = one_hot(pick == 0), one_hot(pick == 112)
    o = LANES_L + 640
    thin[0, :, 0:192] = dot_t(first, margin[...].reshape(192, 128)).astype(BF)
    thin[1, :, 0:192] = dot_t(first, nat[:, inner, o : o + 128].reshape(192, 128)).astype(BF)
    thin[2, :, 0:192] = dot_t(last, nat[:, inner, o + 384 : o + 512].reshape(192, 128)).astype(BF)
    edges = [
        zcopy(9, thin.at[0], strips.at[0, 0:16], -2),
        zcopy(10, thin.at[1], strips.at[1, 0:16], -2),
        zcopy(11, thin.at[2], strips.at[2, 112:128], 2),
    ]
    for copy in edges + second + rest:
        copy.start()

    strips[0, 16:128] = jnp.zeros((112, 256), BF)
    strips[1, 16:128] = jnp.zeros((112, 256), BF)
    strips[2, 0:112] = jnp.zeros((112, 256), BF)
    build_selectors(sel)
    shuffle = row_permutation()
    for load in loads[3:]:
        load.wait()
    build_weights(enc_ref, mix_ref, agg_ref, wenc, wmix, wagg)
    feats[RIGHT + 384 :, :] = jnp.zeros((128, 2304), BF)

    row128 = iota((ROWS, 128), 0)
    col_of = jnp.where(row128 < RIGHT, TILE * t - 9 + row128, TILE * t + 129 + RIGHT - row128)
    valid = (col_of >= 0) & (col_of < 2048)

    def clear(rows, lo, hi):
        size = rows.size if isinstance(rows, pl.Slice) else rows.stop - rows.start
        nat[:, rows, lo:hi] = jnp.zeros((3, size, hi - lo), BF)

    pl.semaphore_wait(near_sem, 2)
    signal(far_sem, zdev(4))
    signal(far_sem, zdev(-4))

    for copy in edges:
        copy.wait()
    same = one_hot(iota((192, 192), 0) == iota((192, 192), 1))
    for i, lane in ((0, 640), (1, LANES_L + 1664), (2, LANES_L)):
        strip = dot_t(same, strips[i, :, 0:192]).astype(BF)
        nat[:, inner, lane : lane + 128] = strip.reshape(3, 64, 128)

    @pl.when(t == 0)
    def _():
        clear(inner, 0, 128)
        clear(inner, LANES_L, LANES_L + 128)
        clear(inner, LANES_L + 640, LANES_L + 1152)

    @pl.when((t == 1) | (t == 2))
    def _():
        clear(inner, LANES_L, LANES_L + 128)

    @pl.when(t == nz - 1)
    def _():
        clear(inner, 640, 768)
        clear(inner, LANES_L + 1664, LANES_L + 1792)

    def arrived(copies, rows):
        for copy in copies:
            copy.wait()

        @pl.when((t == 0) | (t == 1))
        def _():
            clear(rows, LANES_L + 128, LANES_L + 640)

    def rcopy(i, down):
        lo, to = pl.multiple_of(jnp.where(down, 64, 16), 16), pl.multiple_of(jnp.where(down, 0, 80), 16)
        return pltpu.make_async_remote_copy(
            src_ref=nat.at[:, pl.ds(lo, 16)], dst_ref=nat.at[:, pl.ds(to, 16)], send_sem=rsend.at[i], recv_sem=rrecv.at[i],
            device_id={"rows": lax.rem(r + jnp.where(down, 1, nr - 1), nr)}, device_id_type=MESH,
        )

    halos = rcopy(0, ahead), rcopy(1, jnp.logical_not(ahead))

    low = iota((1, 128), 1) < 64
    enc_bias = encb_ref[...]

    def take(w):
        for lo in range(0, LANES, 512):
            x = nat[:, pl.ds(pl.multiple_of(16 * w, 16), 32), lo : lo + 512].reshape(96, 512)
            taken[w, :, lo : lo + 512] = dot(shuffle, x).astype(BF)

    def joined(order):
        return lambda lanes: jnp.concatenate([taken[w, :, lanes] for w in order], axis=0)

    def gather_one(w):
        def store_one(rows, jp, te, to):
            u[w, rows, jp * 128 : (jp + 1) * 128] = jnp.where(low, te, to).astype(BF)

        take(w)
        gather_taps(joined((w, w)), joined((w, w)), sel, store_one)

    def store_rest(rows, jp, te, to):
        lanes = slice(jp * 128, (jp + 1) * 128)
        e, o = te[:, :128], to[:, :128]
        u[0, rows, lanes] = jnp.where(low, e, o).astype(BF)
        u[third_w, rows, lanes] = jnp.where(low, o, e).astype(BF)
        u[4, rows, lanes] = jnp.where(low, te[:, 128:], to[:, 128:]).astype(BF)

    arrived(middle, slice(32, 64))

    def gather_first():
        gather_one(2)

    def gather_second():
        arrived(second, pl.ds(pl.multiple_of(jnp.where(ahead, 64, 16), 16), 16))
        halos[0].start()
        gather_one(first_w)
        arrived(rest, pl.ds(pl.multiple_of(jnp.where(ahead, 16, 64), 16), 16))
        halos[1].start()
        pl.semaphore_wait(far_sem, 2)

    def gather_rest():
        for copy in halos:
            copy.wait()

        @pl.when(r == 0)
        def _():
            clear(slice(0, 16), 0, LANES)

        @pl.when(r == nr - 1)
        def _():
            clear(slice(80, 96), 0, LANES)

        for w in (0, third_w, 4):
            take(w)
        gather_taps(joined((0, third_w, 4, 4)), joined((third_w, 0, 4, 4)), sel, store_rest)

    mix_bias = mixb_ref[...]
    ql = TILE * t - 8 + iota((RIGHT, 128), 0)
    valid_l = (ql >= 0) & (ql < 2048)
    qr = TILE * t + 128 - iota((392, 128), 0)
    valid_r = (qr >= 0) & (qr < 2048)

    def mix(s):
        lanes = pl.ds(pl.multiple_of(s * 256, 256), 512)
        x = lower[:, lanes]
        z = dot(x, wmix[...])
        zs[:, 0:256] = z[:, 0:256]
        zs[:, 256:512] = z[:, 256:512] + x[:, 128:384].astype(F32)
        zs[:, 512:768] = z[:, 512:768]
        for k in range(2):
            a, b, c = (slice(i * 256 + k * 128, i * 256 + (k + 1) * 128) for i in range(3))
            dst = pl.ds(pl.multiple_of(s * 256 + k * 128, 128), 128)
            fl = zs[0:144, a] + zs[1:145, b] + zs[2:146, c] + mix_bias
            feats[0:144, dst] = jnp.where(valid_l, fl, 0.0).astype(BF)
            o = RIGHT
            fr = zs[o + 2 : o + 394, a] + zs[o + 1 : o + 393, b] + zs[o : o + 392, c] + mix_bias
            feats[o : o + 392, dst] = jnp.where(valid_r, fr, 0.0).astype(BF)

        @pl.when((r == 0) & (s == 0))
        def _():
            feats[0:RIGHT, 0:128] = jnp.zeros((RIGHT, 128), BF)

        @pl.when((r == nr - 1) & (s == 8))
        def _():
            feats[0:RIGHT, 2176:2304] = jnp.zeros((RIGHT, 128), BF)

    def correlate(n):
        lanes = pl.ds(pl.multiple_of(n * 128, 128), 128)
        scores = dot_t(feats[0:RIGHT, lanes], feats[RIGHT : RIGHT + 512, lanes])
        turned = jnp.concatenate(
            [
                pltpu.roll(scores[lo:hi, :wide], (wide - 136 + lo) % wide, 1, stride=1, stride_axis=0)[:, :DISP]
                for lo, hi, wide in ((0, 64, 512), (64, 128, 384), (128, 144, 384))
            ],
            axis=0,
        )
        dst = pl.ds(pl.multiple_of(n * DISP, DISP), DISP)
        volume[:, dst] = (turned * (1.0 / math.sqrt(128.0))).astype(BF)

    agg_bias = aggb_ref[...]
    place = pl.ds(pl.multiple_of(t * TILE, TILE), TILE)

    def send(p):
        return pltpu.make_async_remote_copy(
            src_ref=stage.at[p], dst_ref=out_ref.at[0, place], send_sem=osend.at[p], recv_sem=orecv.at[m],
            device_id={"cols": p}, device_id_type=MESH,
        )

    def aggregate(s):
        lanes = pl.ds(pl.multiple_of(s * 512, 512), 1024)
        zs[0:RIGHT] = dot(volume[:, lanes], wagg[...])
        for k in range(2):
            a, b, c = (slice(i * 256 + k * 128, i * 256 + (k + 1) * 128) for i in range(3))
            p = 2 * s + k
            stage[p] = (zs[7:135, a] + zs[8:136, b] + zs[9:137, c] + agg_bias).astype(BF)

            @pl.when(p != m)
            def _():
                send(p).start()

    def step(i, carry):
        s = jnp.where(ahead, lax.rem(i + 4, 9), jnp.where(i < 5, 4 - i, i))

        @pl.when(i == 0)
        def _():
            gather_first()

        @pl.when(i == 1)
        def _():
            gather_second()

        @pl.when(i == 3)
        def _():
            gather_rest()

        @pl.when((i == 0) | (i == 1) | (i == 3) | (i == 5) | (i == jnp.where(ahead, 6, 7)))
        def _():
            late = jnp.where(ahead, jnp.where(i == 3, 4, jnp.where(i == 5, 0, 1)), jnp.where(i == 3, 0, jnp.where(i == 5, 3, 4)))
            w = jnp.where(i == 0, 2, jnp.where(i == 1, first_w, late))
            kind = jnp.where(w == third_w, 1, 0)
            compute_lower(u.at[w], wenc.at[kind], enc_bias, valid, lower, 512 * w)

            @pl.when((r == 0) & (w == 0))
            def _():
                lower[:, 0:256] = jnp.zeros((ROWS, 256), BF)

            @pl.when((r == nr - 1) & (w == 4))
            def _():
                lower[:, 2304:2560] = jnp.zeros((ROWS, 256), BF)

        mix(s)
        correlate(2 * s)
        correlate(2 * s + 1)

        below_s = ahead | (i > 4)

        @pl.when((i > 0) & ((s > 0) | jnp.logical_not(below_s)))
        def _():
            aggregate(jnp.where(below_s, s - 1, s))

        return carry

    lax.fori_loop(0, 9, step, 0)

    @pl.when(ahead)
    def _():
        aggregate(3)

    keep = pltpu.make_async_copy(stage.at[m], out_ref.at[0, place], own_sem)
    keep.start()
    keep.wait()

    def finish(p, carry):
        @pl.when(p != m)
        def _():
            send(p).wait_send()
            src = pl.ds(pl.multiple_of(lax.rem(p + 1, nz) * TILE, TILE), TILE)
            pltpu.make_async_remote_copy(
                src_ref=stage.at[p], dst_ref=out_ref.at[0, src], send_sem=osend.at[p], recv_sem=orecv.at[p],
                device_id={"cols": p}, device_id_type=MESH,
            ).wait_recv()

        return carry

    lax.fori_loop(0, 16, finish, 0)


def local(images, enc_weight, enc_bias, mix_weight, mix_bias, agg_weight, agg_bias):
    vmem, hbm = pl.BlockSpec(memory_space=pltpu.VMEM), pl.BlockSpec(memory_space=pltpu.HBM)
    return pl.pallas_call(
        kernel,
        out_shape=jax.ShapeDtypeStruct((1, 2048, 128), BF),
        in_specs=[hbm, hbm, vmem, hbm, vmem, hbm, vmem],
        out_specs=hbm,
        scratch_shapes=[
            pltpu.VMEM((3, 64, 128), BF),
            pltpu.VMEM((192, 128), BF),
            pltpu.VMEM((3, 3, 128, 128), BF),
            pltpu.VMEM((3, 3, 256, 128), BF),
            pltpu.VMEM((3, 96, LANES), BF),
            pltpu.VMEM((3, 16, 256), BF),
            pltpu.VMEM((3, 128, 256), BF),
            pltpu.VMEM((5, 64, LANES), BF),
            pltpu.VMEM((2, 512, 384), BF),
            pltpu.VMEM((2, 512, 512), BF),
            pltpu.VMEM((512, 768), BF),
            pltpu.VMEM((1024, 768), BF),
            pltpu.VMEM((5, ROWS, 512), BF),
            pltpu.VMEM((ROWS, 2560), BF),
            pltpu.VMEM((ROWS, 768), F32),
            pltpu.VMEM((RIGHT + 512, 2304), BF),
            pltpu.VMEM((RIGHT, 18 * DISP), BF),
            pltpu.VMEM((16, 128, 128), BF),
            pltpu.SemaphoreType.DMA((6,)),
            pltpu.SemaphoreType.DMA((12,)),
            pltpu.SemaphoreType.DMA((12,)),
            pltpu.SemaphoreType.DMA((2,)),
            pltpu.SemaphoreType.DMA((2,)),
            pltpu.SemaphoreType.DMA((16,)),
            pltpu.SemaphoreType.DMA((16,)),
            pltpu.SemaphoreType.DMA,
            pltpu.SemaphoreType.REGULAR,
            pltpu.SemaphoreType.REGULAR,
        ],
        compiler_params=pltpu.CompilerParams(
            collective_id=0, has_side_effects=True, vmem_limit_bytes=60 * 1024 * 1024
        ),
        name="stereo",
    )(
        images,
        enc_weight.reshape(192, 128),
        enc_bias.reshape(1, 128),
        mix_weight,
        mix_bias.reshape(1, 128),
        agg_weight,
        agg_bias.reshape(1, 128),
    )


def solution(mesh):
    return jax.shard_map(
        local,
        mesh=mesh,
        in_specs=(P(None, None, "rows", "cols"), P(), P(), P(), P(), P(), P()),
        out_specs=P(("rows", "cols"), None, None),
        check_vma=False,
    )
```
